32 devices in a mesh: gx: 4 (over x, core), gy: 8 (over z, y).
Axes of the slice: x: 2, y: 2, z: 4, core: 2. Of those that a mesh axis runs over, the one named last changes fastest.
Arguments:
- direct: float32 [4, 4, 8, 1024], P(None, 'gx', 'gy'), may hold values from 0 to 1
- omega: float32 [3, 4, 8, 1024], P(None, 'gx', 'gy'), may hold values from 0.1 to 0.9
- band_sun: float32 [3, 4], replicated, may hold values from 0.5 to 2
- air_temp: float32 [4], replicated, may hold values from 15 to 35
- vcmax: float32 [4, 8, 1024], P('gx', 'gy'), may hold values from 0.4 to 1.6
- self_view: bfloat16 [4, 8, 1024, 1024], P('gx', 'gy'), may hold values from 1e-07 to 0.0401
- near_view: bfloat16 [4, 8, 8, 1024, 1024], P('gx', 'gy'), may hold values from 1e-07 to 0.0401
- near_ids: int32 [4, 8, 8], P('gx', 'gy'), may hold values from 0 to 31, as said below
- organ_of_patch: int32 [4, 8, 1024], P('gx', 'gy'), may hold values from 0 to 1279
- organ_plant: int32 [1280], replicated, may hold values from 0 to 159
Outputs:
- assimilation: float32 [4, 8, 1024], P('gx', 'gy')
- organ_carbon: float32 [1280], P(('gx', 'gy'))
- plant_carbon: float32 [160], P(('gx', 'gy'))
The draws below stay inside these ranges and needn't reach their ends.
Inputs may be any that keep to these rules, and one draw needn't show every extreme that they name: `near_ids`: the 8 ids of a block are distinct, differ from the block itself, and lie within two block rows and two block columns of it.
All inputs are finite; a program needn't handle non-finite values.
Results may differ from the reference program's by a relative error of at most 0.0003.
Values may be sent and summed in bfloat16 or wider, within the bound.
A program may use at most 64 MiB of HBM per device.

```python
import math
import jax
import jax.numpy as jnp
import numpy as np
from jax import lax

PB = 1024
NEAR = 8
BANDS = 3
SUNS = 4
SWEEPS = 2
NR = 4
NC = 8
PLANTS = 160
ORGANS = 1280


def draw_near_ids(key, part):
    key = jax.random.fold_in(key, 11)
    offsets = np.array([(a, b) for a in range(-2, 3) for b in range(-2, 3) if (a, b) != (0, 0)], dtype=np.int32)
    step_row = jnp.asarray(offsets[:, 0])
    step_col = jnp.asarray(offsets[:, 1])
    row_pos = jnp.arange(NR, dtype=jnp.int32)[:, None, None] + step_row[None, None, :]
    col_pos = jnp.arange(NC, dtype=jnp.int32)[None, :, None] + step_col[None, None, :]
    inside = (row_pos >= 0) & (row_pos < NR) & (col_pos >= 0) & (col_pos < NC)
    inside = jnp.broadcast_to(inside, (NR, NC, 24))
    label = jnp.arange(24, dtype=jnp.int32)
    randbits = jax.random.randint(key, (NR, NC, 24), 0, 1 << 20, dtype=jnp.int32)
    score = jnp.where(inside, randbits * 32 + label, -1 - label)
    unused, picked = lax.top_k(score, 8)
    target = jnp.broadcast_to(row_pos * NC + col_pos, (NR, NC, 24))
    return jnp.take_along_axis(target, picked, axis=-1).astype(jnp.int32)


def view_pieces(key, shape):
    key_mark, key_low, key_high = jax.random.split(key, 3)
    marked = jax.random.randint(key_mark, shape, 0, PB, dtype=jnp.int32) < 2
    low_u = jax.random.uniform(key_low, shape, jnp.float32)
    background = 1e-07 + low_u * (0.00025 - 1e-07)
    high_u = jax.random.uniform(key_high, shape, jnp.float32)
    return (marked, background, high_u)


def draw_self_view(key, part):
    key = jax.random.fold_in(key, 21)
    marked, background, high_u = view_pieces(key, (NR, NC, PB, PB))
    strong = jnp.exp(jnp.log(0.005) + high_u * jnp.log(8.0))
    return jnp.where(marked, strong, background).astype(jnp.bfloat16)


def draw_near_view(key, part):
    key = jax.random.fold_in(key, 23)
    marked, background, high_u = view_pieces(key, (NR, NC, NEAR, PB, PB))
    strong = jnp.exp(jnp.log(0.005) + high_u * jnp.log(8.0))
    return jnp.where(marked, strong, background).astype(jnp.bfloat16)


def plant(entries, stream_key, low, largest):
    place = [jax.random.randint(jax.random.fold_in(stream_key, axis), (), 0, length) for axis, length in enumerate(entries.shape)]
    main_axis = entries.shape.index(max(entries.shape))
    neighbour = place[:main_axis] + [(place[main_axis] + 1) % entries.shape[main_axis]] + place[main_axis + 1:]
    return entries.at[tuple(place)].set(low).at[tuple(neighbour)].set(largest)


def level_of(rng, shape, shards, least, high):
    factor_of = 1.0
    for dim, shards_of in shards:
        heights = jax.random.uniform(jax.random.fold_in(jax.random.fold_in(rng, 6), dim), (shards_of,), jnp.float32, least / len(shards), high / len(shards))
        factor_of = factor_of * jnp.repeat(jnp.exp(heights), shape[dim] // shards_of).reshape((-1,) + (1,) * (len(shape) - 1 - dim))
    return factor_of


def setup_inputs(seed: int = 0) -> dict:
    seeds = jax.random.split(jax.random.key(seed), 11)
    direct = jnp.clip(1.0 * jax.random.uniform(seeds[0], (SUNS, NR, NC, PB), jnp.float32) ** level_of(seeds[0], (SUNS, NR, NC, PB), ((1, 4), (2, 8)), -0.2, 0.2), 0.0, 1.0)
    omega = jnp.clip(0.1 + 0.79999997 * jax.random.uniform(seeds[1], (BANDS, NR, NC, PB), jnp.float32) ** level_of(seeds[1], (BANDS, NR, NC, PB), ((1, 4), (2, 8)), -0.2, 0.2), 0.1, 0.9)
    band_sun = jnp.clip(jnp.exp(jax.random.uniform(seeds[2], (BANDS, SUNS), jnp.float32, math.log(0.5), math.log(2.0))), 0.5, 2.0)
    air_temp = jnp.clip(jax.random.uniform(seeds[3], (SUNS,), jnp.float32, 15.0, 35.0), 15.0, 35.0)
    vcmax = jnp.clip(jnp.exp(math.log(1.6) - 1.3862944 * jax.random.uniform(seeds[4], (NR, NC, PB), jnp.float32) ** level_of(seeds[4], (NR, NC, PB), ((0, 4), (1, 8)), -0.2, 0.2)), 0.4, 1.6)
    self_view = draw_self_view(jax.random.fold_in(seeds[10], 71), 0)
    near_view = draw_near_view(jax.random.fold_in(seeds[10], 71), 0)
    near_ids = draw_near_ids(jax.random.fold_in(seeds[10], 71), 0)
    organ_of_patch = plant(jax.random.randint(seeds[8], (NR, NC, PB), 0, ORGANS), jax.random.fold_in(seeds[8], 1), 0, ORGANS - 1).astype(jnp.int32)
    organ_plant = plant(jax.random.randint(seeds[9], (ORGANS,), 0, PLANTS), jax.random.fold_in(seeds[9], 1), 0, PLANTS - 1).astype(jnp.int32)
    return {"direct": direct, "omega": omega, "band_sun": band_sun, "air_temp": air_temp, "vcmax": vcmax, "self_view": self_view, "near_view": near_view, "near_ids": near_ids, "organ_of_patch": organ_of_patch, "organ_plant": organ_plant}


def assimilate(absorbed, vcmax, air_temp):
    shape = (air_temp.shape[0],) + (1,) * (absorbed.ndim - 2)
    heat = absorbed[1] + absorbed[2]
    leaf_temp = air_temp.reshape(shape) + 6.0 * heat
    capacity = vcmax[None] * jnp.exp(0.07 * (leaf_temp - 25.0))
    jmax = 1.7 * capacity
    light = 1.5 * absorbed[0]
    total = light + jmax
    elec = (total - jnp.sqrt(total * total - 2.8 * light * jmax)) / 1.4
    carbox = capacity * (0.7 - 0.05) / (0.7 + 0.5)
    electron = elec * (0.7 - 0.05) / (0.7 + 0.1)
    net_rate = jnp.minimum(carbox, electron) - 0.015 * capacity
    return 0.25 * lax.optimization_barrier(jnp.sum(net_rate, axis=0))

def reference(direct, omega, band_sun, air_temp, vcmax, self_view, near_view, near_ids, organ_of_patch, organ_plant):
    blocks = NR * NC
    width = PB
    source = (band_sun[:, :, None, None, None] * direct[None]).reshape(BANDS * SUNS, blocks, width)
    albedo = jnp.broadcast_to(omega.reshape(BANDS, 1, blocks, width), (BANDS, SUNS, blocks, width)).reshape(BANDS * SUNS, blocks, width)
    self_flat = self_view.reshape(blocks, width, width)
    near_flat = near_view.reshape(blocks, NEAR, width, width)
    ids_flat = near_ids.reshape(blocks, NEAR).astype(jnp.int32)
    order = jnp.arange(blocks, dtype=jnp.int32)
    current = source
    scattered = source
    for sweep in range(SWEEPS):
        sent = current.astype(jnp.bfloat16)

        def one_block(items):
            own_view, far_view, neighbours, index = items
            own = lax.dynamic_index_in_dim(sent, index, 1, False).astype(jnp.float32)
            far = jnp.take(sent, neighbours, axis=1).astype(jnp.float32)
            result = jnp.einsum('pq,kq->kp', own_view.astype(jnp.float32), own)
            return result + jnp.einsum('npq,knq->kp', far_view.astype(jnp.float32), far)
        scattered = jnp.transpose(lax.map(one_block, (self_flat, near_flat, ids_flat, order)), (1, 0, 2))
        current = source + albedo * scattered
    absorbed = ((1.0 - albedo) * (source + scattered)).reshape(BANDS, SUNS, blocks, width)
    assimilation = assimilate(absorbed, vcmax.reshape(blocks, width), air_temp)
    organ_carbon = 0.25 * jax.ops.segment_sum(assimilation.reshape(-1), organ_of_patch.reshape(-1), num_segments=ORGANS)
    plant_carbon = jax.ops.segment_sum(organ_carbon, organ_plant, num_segments=PLANTS) / 8.0
    return (assimilation.reshape(NR, NC, PB), organ_carbon, plant_carbon)
```

```python
import functools

import jax
import jax.numpy as jnp
from jax import lax
from jax.experimental import pallas as pl
from jax.experimental.pallas import tpu as pltpu
from jax.sharding import PartitionSpec as P

REACH = 2
SIDE = 2 * REACH + 1
SLOTS = SIDE * SIDE
HALVES = 2
PLANT_LANE = 64
MESH = pl.DeviceIdType.MESH
NT = (((1,), (1,)), ((), ()))


def nt_dot(left, right):
    return lax.dot_general(left, right, NT, preferred_element_type=jnp.float32)


def column(values, rows, width):
    index = lax.broadcasted_iota(jnp.int32, (rows, width), 0)
    out = jnp.full((rows, width), values[0], jnp.float32)
    for i in range(1, rows):
        out = jnp.where(index == i, values[i], out)
    return out


def kernel(
    rows, cols, organs, plants,
    direct, omega, band_sun, air_temp, vcmax, self_view, near_view, near_ids, organ_ref, table_ref,
    assim_ref, share_ref,
    views, own, tiles, msg1, recv1, msg2a, msg2b, recv2a, recv2b,
    table, plant_row, dest_org, dest_pl, lane_org, lane_pl, part, gathered,
    load_sem, send1, got1, send2a, got2a, send2b, got2b, send3, got3,
):
    suns = direct.shape[0]
    bands = omega.shape[0]
    near = near_view.shape[2]
    width = vcmax.shape[-1]
    half = width // HALVES
    quarter = half // 4
    ndev = rows * cols
    row = lax.axis_index("gx")
    col = lax.axis_index("gy")
    me = row * cols + col

    loads = []
    for h in range(HALVES):
        span = pl.ds(h * half, half)
        for n in range(near + 1):
            source = self_view.at[0, 0, span] if n == 0 else near_view.at[0, 0, n - 1, span]
            loads.append(pltpu.make_async_copy(source, views.at[n, span], load_sem.at[h, n]))
    for load in loads:
        load.start()

    barrier = pltpu.get_barrier_semaphore()

    def greet(k, carry):
        peer = lax.rem(me + k, ndev)
        pl.semaphore_signal(barrier, inc=1, device_id=(peer // cols, lax.rem(peer, cols)), device_id_type=MESH)
        return carry

    lax.fori_loop(1, ndev, greet, 0)

    row_lo, row_hi = jnp.maximum(row - REACH, 0), jnp.minimum(row + REACH, rows - 1)
    col_lo, col_hi = jnp.maximum(col - REACH, 0), jnp.minimum(col + REACH, cols - 1)

    def each_neighbour(body):
        def by_row(r, carry):
            def by_col(c, inner):
                @pl.when((r != row) | (c != col))
                def _():
                    body(r, c)
                return inner
            return lax.fori_loop(col_lo, col_hi + 1, by_col, carry)
        lax.fori_loop(row_lo, row_hi + 1, by_row, 0)

    def exchange(message, slots, send_sem, got_sem, r, c, outgoing):
        there = (row - r + REACH) * SIDE + (col - c + REACH)
        here = (r - row + REACH) * SIDE + (c - col + REACH)
        return pltpu.make_async_remote_copy(
            src_ref=message, dst_ref=slots.at[there if outgoing else here],
            send_sem=send_sem.at[there], recv_sem=got_sem.at[there if outgoing else here],
            device_id=(r, c), device_id_type=MESH,
        )

    def send(*buffers):
        each_neighbour(lambda r, c: exchange(*buffers, r, c, True).start())

    def receive(*buffers):
        each_neighbour(lambda r, c: exchange(*buffers, r, c, False).wait_recv())

    def sent(*buffers):
        each_neighbour(lambda r, c: exchange(*buffers, r, c, True).wait_send())

    first = (msg1, recv1, send1, got1)
    second = ((msg2a, recv2a, send2a, got2a), (msg2b, recv2b, send2b, got2b))

    own[...] = jnp.zeros_like(own)
    for s in range(suns):
        own[s:s + 1, :] = direct[s, 0]
    for b in range(bands):
        own[suns + b:suns + b + 1, :] = omega[b, 0]
    own_tile = own[...]
    msg1[...] = jnp.concatenate([own_tile[:, :half], own_tile[:, half:]], axis=0).astype(jnp.bfloat16)
    tiles[0] = own_tile

    pl.semaphore_wait(barrier, ndev - 1)
    send(*first)

    table[...] = jnp.zeros_like(table)
    table[0:table_ref.shape[0], :] = table_ref[...]
    entries = table[...]
    level = lax.broadcasted_iota(jnp.int32, entries.shape, 0)
    for j in range(width // 128):
        ids = organ_ref[0, :, j * 128:(j + 1) * 128]
        low = jnp.broadcast_to(ids & 127, entries.shape)
        picked = jnp.take_along_axis(entries, low, axis=1)
        picked = jnp.where(level == (ids >> 7), picked, 0).astype(jnp.float32)
        plant_row[:, j * 128:(j + 1) * 128] = jnp.sum(picked, axis=0, keepdims=True)
    for ids, total, base, dest_ref, lane_ref in (
        (organ_ref[0].astype(jnp.float32), organs, 0, dest_org, lane_org),
        (plant_row[...], plants, PLANT_LANE, dest_pl, lane_pl),
    ):
        share = total // ndev
        dest = jnp.floor((ids + 0.5) * (1.0 / share))
        lane = ids - dest * share + base
        at_row = lax.broadcasted_iota(jnp.int32, (ndev, width), 0).astype(jnp.float32)
        dest_ref[...] = jnp.where(at_row == dest, 1.0, 0.0)
        at_lane = lax.broadcasted_iota(jnp.int32, (128, width), 0).astype(jnp.float32)
        lane_ref[...] = jnp.where(at_lane == lane, 1.0, 0.0).astype(jnp.bfloat16)

    slot_of = []
    for n in range(near):
        block = near_ids[0, 0, n]
        place = (block // cols - row + REACH) * SIDE + (lax.rem(block, cols) - col + REACH)
        slot_of.append(jnp.clip(place, 0, SLOTS - 1))

    own_low = own_tile.astype(jnp.bfloat16)
    once = []
    for h in range(HALVES):
        span = slice(h * half, (h + 1) * half)
        loads[h * (near + 1)].wait()
        total = nt_dot(own_low, views[0, span, :])
        if h == 0:
            receive(*first)
            for n in range(near):
                arrived = recv1[slot_of[n]].astype(jnp.float32)
                tiles[n + 1] = jnp.concatenate([arrived[0:8], arrived[8:16]], axis=1)
        for n in range(1, near + 1):
            loads[h * (near + 1) + n].wait()
            total = total + nt_dot(tiles[n].astype(jnp.bfloat16), views[n, span, :])
        total = total[0:suns]
        once.append(total)
        packed = jnp.concatenate([total[:, i * quarter:(i + 1) * quarter] for i in range(4)], axis=0)
        second[h][0][...] = packed.astype(jnp.bfloat16)
        send(*second[h])

    def second_input(n, h, light):
        span = slice(h * half, (h + 1) * half)
        scaled = [tiles[n, suns + b:suns + b + 1, span] * light for b in range(bands)]
        scaled.append(jnp.zeros((16 - suns * bands, half), jnp.float32))
        return jnp.concatenate(scaled, axis=0).astype(jnp.bfloat16)

    twice = None
    for h in range(HALVES):
        term = nt_dot(second_input(0, h, once[h]), views[0, :, h * half:(h + 1) * half])
        twice = term if twice is None else twice + term
    for h in range(HALVES):
        receive(*second[h])
        for n in range(1, near + 1):
            arrived = second[h][1][slot_of[n - 1]].astype(jnp.float32)
            light = jnp.concatenate([arrived[4 * i:4 * i + 4] for i in range(4)], axis=1)
            twice = twice + nt_dot(second_input(n, h, light), views[n, :, h * half:(h + 1) * half])

    base = own[0:suns, :] + jnp.concatenate(once, axis=1)
    absorbed = []
    for b in range(bands):
        factor = column([band_sun[b, s] for s in range(suns)], suns, width)
        gathered_light = factor * (base + twice[b * suns:(b + 1) * suns])
        absorbed.append((1.0 - own[suns + b:suns + b + 1, :]) * gathered_light)
    air = column([air_temp[s] for s in range(suns)], suns, width)
    leaf_temp = air + 6.0 * (absorbed[1] + absorbed[2])
    capacity = vcmax[0] * jnp.exp(0.07 * (leaf_temp - 25.0))
    jmax = 1.7 * capacity
    light = 1.5 * absorbed[0]
    total = light + jmax
    elec = (total - jnp.sqrt(total * total - 2.8 * light * jmax)) * (1.0 / 1.4)
    carbox = capacity * ((0.7 - 0.05) / (0.7 + 0.5))
    electron = elec * ((0.7 - 0.05) / (0.7 + 0.1))
    net_rate = jnp.minimum(carbox, electron) - 0.015 * capacity
    assim = 0.25 * jnp.sum(net_rate, axis=0, keepdims=True)
    assim_ref[0] = assim

    high = assim.astype(jnp.bfloat16).astype(jnp.float32)
    rest = assim - high
    middle = rest.astype(jnp.bfloat16).astype(jnp.float32)
    low = rest - middle
    sums = None
    for dest_ref, lane_ref in ((dest_org, lane_org), (dest_pl, lane_pl)):
        dest = dest_ref[...]
        stacked = jnp.concatenate([dest * high, dest * middle, dest * low], axis=0).astype(jnp.bfloat16)
        found = nt_dot(stacked, lane_ref[...])
        sums = found if sums is None else sums + found
    sums = sums[0:ndev] + sums[ndev:2 * ndev] + sums[2 * ndev:3 * ndev]
    part[...] = sums

    def hand(k, outgoing):
        peer = lax.rem(me + k, ndev)
        origin = me if outgoing else peer
        return pltpu.make_async_remote_copy(
            src_ref=part.at[pl.ds(peer, 1)], dst_ref=gathered.at[pl.ds(origin, 1)],
            send_sem=send3.at[peer], recv_sem=got3.at[origin],
            device_id=(peer // cols, lax.rem(peer, cols)), device_id_type=MESH,
        )

    def over_peers(act):
        def step(k, carry):
            act(k)
            return carry
        lax.fori_loop(1, ndev, step, 0)

    over_peers(lambda k: hand(k, True).start())
    gathered[pl.ds(me, 1), :] = part[pl.ds(me, 1), :]
    sent(*first)
    sent(*second[0])
    sent(*second[1])
    over_peers(lambda k: hand(k, False).wait_recv())
    share_ref[...] = jnp.sum(gathered[...], axis=0, keepdims=True)
    over_peers(lambda k: hand(k, True).wait_send())


def shards(
    direct, omega, band_sun, air_temp, vcmax, self_view, near_view, near_ids, organ_of_patch, organ_plant,
    *, rows, cols, plants,
):
    ndev = rows * cols
    organs = organ_plant.shape[0]
    near = near_ids.shape[-1]
    width = vcmax.shape[-1]
    levels = organs // 128
    padded = (levels + 7) // 8 * 8
    vmem = pl.BlockSpec(memory_space=pltpu.VMEM)
    smem = pl.BlockSpec(memory_space=pltpu.SMEM)
    hbm = pl.BlockSpec(memory_space=pl.ANY)
    f32, bf16 = jnp.float32, jnp.bfloat16
    slot_sems = pltpu.SemaphoreType.DMA((SLOTS,))
    peer_sems = pltpu.SemaphoreType.DMA((ndev,))
    assimilation, share = pl.pallas_call(
        functools.partial(kernel, rows, cols, organs, plants),
        out_shape=(
            jax.ShapeDtypeStruct((1, 1, width), f32),
            jax.ShapeDtypeStruct((1, 128), f32),
        ),
        in_specs=[vmem, vmem, smem, smem, vmem, hbm, hbm, smem, vmem, vmem],
        out_specs=(vmem, vmem),
        scratch_shapes=[
            pltpu.VMEM((near + 1, width, width), bf16),
            pltpu.VMEM((8, width), f32),
            pltpu.VMEM((near + 1, 8, width), f32),
            pltpu.VMEM((16, width // 2), bf16),
            pltpu.VMEM((SLOTS, 16, width // 2), bf16),
            pltpu.VMEM((16, width // 8), bf16),
            pltpu.VMEM((16, width // 8), bf16),
            pltpu.VMEM((SLOTS, 16, width // 8), bf16),
            pltpu.VMEM((SLOTS, 16, width // 8), bf16),
            pltpu.VMEM((padded, 128), jnp.int32),
            pltpu.VMEM((1, width), f32),
            pltpu.VMEM((ndev, width), f32),
            pltpu.VMEM((ndev, width), f32),
            pltpu.VMEM((128, width), bf16),
            pltpu.VMEM((128, width), bf16),
            pltpu.VMEM((ndev, 128), f32),
            pltpu.VMEM((ndev, 128), f32),
            pltpu.SemaphoreType.DMA((HALVES, near + 1)),
            slot_sems, slot_sems, slot_sems, slot_sems, slot_sems, slot_sems,
            peer_sems, peer_sems,
        ],
        compiler_params=pltpu.CompilerParams(
            collective_id=0, has_side_effects=True, vmem_limit_bytes=56 * 2**20
        ),
        name="canopy",
    )(
        direct, omega, band_sun, air_temp, vcmax, self_view, near_view, near_ids, organ_of_patch,
        organ_plant.reshape(levels, 128),
    )
    organ_share, plant_share = organs // ndev, plants // ndev
    organ_carbon = 0.25 * share[0, :organ_share]
    plant_carbon = share[0, PLANT_LANE:PLANT_LANE + plant_share] / 32.0
    return assimilation, organ_carbon, plant_carbon


def solution(mesh):
    rows, cols = mesh.shape["gx"], mesh.shape["gy"]

    def whole(*args):
        plants = args[9].shape[0] // 8
        return jax.shard_map(
            functools.partial(shards, rows=rows, cols=cols, plants=plants),
            mesh=mesh,
            in_specs=(
                P(None, "gx", "gy", None),
                P(None, "gx", "gy", None),
                P(),
                P(),
                P("gx", "gy", None),
                P("gx", "gy", None, None),
                P("gx", "gy", None, None, None),
                P("gx", "gy", None),
                P("gx", "gy", None),
                P(),
            ),
            out_specs=(P("gx", "gy", None), P(("gx", "gy")), P(("gx", "gy"))),
            check_vma=False,
        )(*args)

    return whole
```

```python
import functools

import jax
import jax.numpy as jnp
from jax import lax
from jax.experimental import pallas as pl
from jax.experimental.pallas import tpu as pltpu
from jax.sharding import PartitionSpec as P

REACH = 2
SIDE = 2 * REACH + 1
SLOTS = SIDE * SIDE
HALVES = 2
PLANT_LANE = 64
MESH = pl.DeviceIdType.MESH
NT = (((1,), (1,)), ((), ()))


def nt_dot(left, right):
    return lax.dot_general(left, right, NT, preferred_element_type=jnp.float32)


def column(values, rows, width):
    index = lax.broadcasted_iota(jnp.int32, (rows, width), 0)
    out = jnp.full((rows, width), values[0], jnp.float32)
    for i in range(1, rows):
        out = jnp.where(index == i, values[i], out)
    return out


def kernel(
    rows, cols, organs, plants,
    direct, omega, band_sun_in, air_temp_in, vcmax_in, self_view, near_view, near_ids_in, organ_in, table_in,
    assim_ref, share_ref,
    views, own, tiles, msg1, msg0, recv1, recv0, msg2a, msg2b, recv2a, recv2b,
    table, plant_row, dest_org, dest_pl, lane_org, lane_pl, part, gathered,
    band_sun, air_temp, vcmax, near_ids, organ_ref,
    load_sem, small_sem, send1, got1, send0, got0, send2a, got2a, send2b, got2b, send3, got3,
):
    suns = direct.shape[0]
    bands = omega.shape[0]
    near = near_view.shape[2]
    width = vcmax.shape[-1]
    levels = table_in.shape[0]
    half = width // HALVES
    quarter = half // 4
    ndev = rows * cols
    row = lax.axis_index("gx")
    col = lax.axis_index("gy")
    me = row * cols + col

    own[suns + bands:, :] = jnp.zeros((own.shape[0] - suns - bands, width), jnp.float32)
    table[...] = jnp.zeros_like(table)
    pairs = [(direct.at[s, 0], own.at[pl.ds(s, 1)]) for s in range(suns)]
    pairs += [(omega.at[b, 0], own.at[pl.ds(suns + b, 1)]) for b in range(bands)]
    pairs += [
        (near_ids_in, near_ids), (organ_in, organ_ref), (table_in, table.at[pl.ds(0, levels)]),
        (vcmax_in, vcmax), (band_sun_in, band_sun), (air_temp_in, air_temp),
    ]
    smalls = [pltpu.make_async_copy(a, b, small_sem.at[i]) for i, (a, b) in enumerate(pairs)]
    for small in smalls:
        small.start()
    loads = {}
    for h, n in [(h, 0) for h in range(HALVES)] + [(h, n) for h in range(HALVES) for n in range(1, near + 1)]:
        span = pl.ds(h * half, half)
        source = self_view.at[0, 0, span] if n == 0 else near_view.at[0, 0, n - 1, span]
        loads[h, n] = pltpu.make_async_copy(source, views.at[n, span], load_sem.at[h, n])
        loads[h, n].start()

    barrier = pltpu.get_barrier_semaphore()

    def over_peers(act):
        for i in range(rows):
            r = lax.rem(row + i, rows)

            def step(j, carry, r=r):
                act(r, lax.rem(col + j, cols))
                return carry

            lax.fori_loop(1 if i == 0 else 0, cols, step, 0)

    over_peers(lambda r, c: pl.semaphore_signal(barrier, inc=1, device_id=(r, c), device_id_type=MESH))

    row_lo, row_hi = jnp.maximum(row - REACH, 0), jnp.minimum(row + REACH, rows - 1)
    col_lo, col_hi = jnp.maximum(col - REACH, 0), jnp.minimum(col + REACH, cols - 1)

    def each_neighbour(body):
        def by_row(r, carry):
            def by_col(c, inner):
                @pl.when((r != row) | (c != col))
                def _():
                    body(r, c)
                return inner
            return lax.fori_loop(col_lo, col_hi + 1, by_col, carry)
        lax.fori_loop(row_lo, row_hi + 1, by_row, 0)

    def exchange(message, slots, send_sem, got_sem, r, c, outgoing):
        there = (row - r + REACH) * SIDE + (col - c + REACH)
        here = (r - row + REACH) * SIDE + (c - col + REACH)
        return pltpu.make_async_remote_copy(
            src_ref=message, dst_ref=slots.at[there if outgoing else here],
            send_sem=send_sem.at[there], recv_sem=got_sem.at[there if outgoing else here],
            device_id=(r, c), device_id_type=MESH,
        )

    def send(*buffers):
        each_neighbour(lambda r, c: exchange(*buffers, r, c, True).start())

    def receive(*buffers):
        each_neighbour(lambda r, c: exchange(*buffers, r, c, False).wait_recv())

    def sent(*buffers):
        each_neighbour(lambda r, c: exchange(*buffers, r, c, True).wait_send())

    first = (msg1, recv1, send1, got1)
    albedos = (msg0, recv0, send0, got0)
    second = ((msg2a, recv2a, send2a, got2a), (msg2b, recv2b, send2b, got2b))

    def packed(values):
        step = values.shape[1] // 4
        return jnp.concatenate([values[:, i * step:(i + 1) * step] for i in range(4)], axis=0).astype(jnp.bfloat16)

    def unpacked(message):
        values = message.astype(jnp.float32)
        return jnp.concatenate([values[4 * i:4 * i + 4] for i in range(4)], axis=1)

    for small in smalls[:suns + bands]:
        small.wait()
    own_tile = own[...]
    msg1[...] = packed(own_tile[0:4])
    msg0[...] = packed(own_tile[4:8])

    pl.semaphore_wait(barrier, ndev - 1)
    send(*first)
    send(*albedos)
    for small in smalls[suns + bands:]:
        small.wait()

    entries = table[...]
    level = lax.broadcasted_iota(jnp.int32, entries.shape, 0)
    for j in range(width // 128):
        ids = organ_ref[0, :, j * 128:(j + 1) * 128]
        low = jnp.broadcast_to(ids & 127, entries.shape)
        picked = jnp.take_along_axis(entries, low, axis=1)
        picked = jnp.where(level == (ids >> 7), picked, 0).astype(jnp.float32)
        plant_row[:, j * 128:(j + 1) * 128] = jnp.sum(picked, axis=0, keepdims=True)
    for ids, total, base, dest_ref, lane_ref in (
        (organ_ref[0].astype(jnp.float32), organs, 0, dest_org, lane_org),
        (plant_row[...], plants, PLANT_LANE, dest_pl, lane_pl),
    ):
        share = total // ndev
        dest = jnp.floor((ids + 0.5) * (1.0 / share))
        lane = ids - dest * share + base
        at_row = lax.broadcasted_iota(jnp.int32, (ndev, width), 0).astype(jnp.float32)
        dest_ref[...] = jnp.where(at_row == dest, 1.0, 0.0)
        at_lane = lax.broadcasted_iota(jnp.int32, (128, width), 0).astype(jnp.float32)
        lane_ref[...] = jnp.where(at_lane == lane, 1.0, 0.0).astype(jnp.bfloat16)

    slot_of = []
    for n in range(near):
        block = near_ids[0, 0, n]
        place = (lax.div(block, cols) - row + REACH) * SIDE + (lax.rem(block, cols) - col + REACH)
        slot_of.append(jnp.clip(place, 0, SLOTS - 1))

    own_low = own_tile[0:suns].astype(jnp.bfloat16)
    totals = []
    for h in range(HALVES):
        loads[h, 0].wait()
        totals.append(nt_dot(own_low, views[0, h * half:(h + 1) * half, :]))
    receive(*first)
    for n in range(near):
        tiles[n, 0:4, :] = unpacked(recv1[slot_of[n]])
    once = []
    for h in range(HALVES):
        span = slice(h * half, (h + 1) * half)
        total = totals[h]
        for n in range(1, near + 1):
            loads[h, n].wait()
            total = total + nt_dot(tiles[n - 1, 0:4, :].astype(jnp.bfloat16), views[n, span, :])
        once.append(total)
        second[h][0][...] = packed(total)
        send(*second[h])

    def second_input(tile, h, light):
        span = slice(h * half, (h + 1) * half)
        scaled = [tile[suns + b:suns + b + 1, span] * light for b in range(bands)]
        scaled.append(jnp.zeros((16 - suns * bands, half), jnp.float32))
        return jnp.concatenate(scaled, axis=0).astype(jnp.bfloat16)

    twice = None
    for h in range(HALVES):
        term = nt_dot(second_input(own, h, once[h]), views[0, :, h * half:(h + 1) * half])
        twice = term if twice is None else twice + term
    receive(*albedos)
    for n in range(near):
        tiles[n, 4:8, :] = unpacked(recv0[slot_of[n]])
    for h in range(HALVES):
        receive(*second[h])
        for n in range(1, near + 1):
            light = unpacked(second[h][1][slot_of[n - 1]])
            twice = twice + nt_dot(second_input(tiles.at[n - 1], h, light), views[n, :, h * half:(h + 1) * half])

    base = own[0:suns, :] + jnp.concatenate(once, axis=1)
    absorbed = []
    for b in range(bands):
        factor = column([band_sun[b, s] for s in range(suns)], suns, width)
        gathered_light = factor * (base + twice[b * suns:(b + 1) * suns])
        absorbed.append((1.0 - own[suns + b:suns + b + 1, :]) * gathered_light)
    air = column([air_temp[s] for s in range(suns)], suns, width)
    leaf_temp = air + 6.0 * (absorbed[1] + absorbed[2])
    capacity = vcmax[0] * jnp.exp(0.07 * (leaf_temp - 25.0))
    jmax = 1.7 * capacity
    light = 1.5 * absorbed[0]
    total = light + jmax
    elec = (total - jnp.sqrt(total * total - 2.8 * light * jmax)) * (1.0 / 1.4)
    carbox = capacity * ((0.7 - 0.05) / (0.7 + 0.5))
    electron = elec * ((0.7 - 0.05) / (0.7 + 0.1))
    net_rate = jnp.minimum(carbox, electron) - 0.015 * capacity
    assim = 0.25 * jnp.sum(net_rate, axis=0, keepdims=True)
    assim_ref[0] = assim

    high = assim.astype(jnp.bfloat16).astype(jnp.float32)
    rest = assim - high
    middle = rest.astype(jnp.bfloat16).astype(jnp.float32)
    low = rest - middle
    sums = None
    for dest_ref, lane_ref in ((dest_org, lane_org), (dest_pl, lane_pl)):
        dest = dest_ref[...]
        stacked = jnp.concatenate([dest * high, dest * middle, dest * low], axis=0).astype(jnp.bfloat16)
        found = nt_dot(stacked, lane_ref[...])
        sums = found if sums is None else sums + found
    sums = sums[0:ndev] + sums[ndev:2 * ndev] + sums[2 * ndev:3 * ndev]
    part[...] = sums

    def hand(r, c):
        peer = r * cols + c
        pltpu.make_async_remote_copy(
            src_ref=part.at[pl.ds(peer, 1)], dst_ref=gathered.at[pl.ds(me, 1)],
            send_sem=send3, recv_sem=got3, device_id=(r, c), device_id_type=MESH,
        ).start()

    over_peers(hand)
    pltpu.make_async_copy(part.at[pl.ds(me, 1)], gathered.at[pl.ds(me, 1)], got3).start()
    sent(*first)
    sent(*albedos)
    sent(*second[0])
    sent(*second[1])
    pltpu.make_async_copy(part, gathered, got3).wait()
    share_ref[...] = jnp.sum(gathered[...], axis=0, keepdims=True)
    others = pl.ds(0, ndev - 1)
    pltpu.make_async_copy(part.at[others], gathered.at[others], send3).wait()


def finish(organ_share, plant_share, assim_in, share_in, assim_ref, organ_ref, plant_ref):
    assim_ref[...] = assim_in[...]
    organ_ref[...] = 0.25 * share_in[:, 0:organ_share]
    plant_ref[...] = share_in[:, PLANT_LANE:PLANT_LANE + plant_share] * (1.0 / 32.0)


def shards(
    direct, omega, band_sun, air_temp, vcmax, self_view, near_view, near_ids, organ_of_patch, organ_plant,
    *, rows, cols, plants,
):
    ndev = rows * cols
    organs = organ_plant.shape[0]
    near = near_ids.shape[-1]
    width = vcmax.shape[-1]
    levels = organs // 128
    padded = (levels + 7) // 8 * 8
    vmem = pl.BlockSpec(memory_space=pltpu.VMEM)
    hbm = pl.BlockSpec(memory_space=pl.ANY)
    f32, bf16 = jnp.float32, jnp.bfloat16
    slot_sems = pltpu.SemaphoreType.DMA((SLOTS,))
    assimilation, share = pl.pallas_call(
        functools.partial(kernel, rows, cols, organs, plants),
        out_shape=(
            jax.ShapeDtypeStruct((1, 1, width), f32),
            jax.ShapeDtypeStruct((1, 128), f32),
        ),
        in_specs=[hbm] * 10,
        out_specs=(vmem, vmem),
        scratch_shapes=[
            pltpu.VMEM((near + 1, width, width), bf16),
            pltpu.VMEM((8, width), f32),
            pltpu.VMEM((near, 8, width), f32),
            pltpu.VMEM((16, width // 4), bf16),
            pltpu.VMEM((16, width // 4), bf16),
            pltpu.VMEM((SLOTS, 16, width // 4), bf16),
            pltpu.VMEM((SLOTS, 16, width // 4), bf16),
            pltpu.VMEM((16, width // 8), bf16),
            pltpu.VMEM((16, width // 8), bf16),
            pltpu.VMEM((SLOTS, 16, width // 8), bf16),
            pltpu.VMEM((SLOTS, 16, width // 8), bf16),
            pltpu.VMEM((padded, 128), jnp.int32),
            pltpu.VMEM((1, width), f32),
            pltpu.VMEM((ndev, width), f32),
            pltpu.VMEM((ndev, width), f32),
            pltpu.VMEM((128, width), bf16),
            pltpu.VMEM((128, width), bf16),
            pltpu.VMEM((ndev, 128), f32),
            pltpu.VMEM((ndev, 128), f32),
            pltpu.SMEM(band_sun.shape, f32),
            pltpu.SMEM(air_temp.shape, f32),
            pltpu.VMEM(vcmax.shape, f32),
            pltpu.SMEM(near_ids.shape, jnp.int32),
            pltpu.VMEM(organ_of_patch.shape, jnp.int32),
            pltpu.SemaphoreType.DMA((HALVES, near + 1)),
            pltpu.SemaphoreType.DMA((16,)),
            slot_sems, slot_sems, slot_sems, slot_sems, slot_sems, slot_sems, slot_sems, slot_sems,
            pltpu.SemaphoreType.DMA, pltpu.SemaphoreType.DMA,
        ],
        compiler_params=pltpu.CompilerParams(
            collective_id=0, has_side_effects=True, vmem_limit_bytes=56 * 2**20
        ),
        name="canopy",
    )(
        direct, omega, band_sun, air_temp, vcmax, self_view, near_view, near_ids, organ_of_patch,
        organ_plant.reshape(levels, 128),
    )
    organ_share, plant_share = organs // ndev, plants // ndev
    assimilation, organ_carbon, plant_carbon = pl.pallas_call(
        functools.partial(finish, organ_share, plant_share),
        out_shape=(
            jax.ShapeDtypeStruct((1, 1, width), f32),
            jax.ShapeDtypeStruct((1, organ_share), f32),
            jax.ShapeDtypeStruct((1, plant_share), f32),
        ),
        in_specs=[vmem, vmem],
        out_specs=(vmem, vmem, vmem),
        compiler_params=pltpu.CompilerParams(vmem_limit_bytes=60 * 2**20),
        name="finish",
    )(assimilation, share)
    return assimilation, organ_carbon.reshape(-1), plant_carbon.reshape(-1)


def solution(mesh):
    rows, cols = mesh.shape["gx"], mesh.shape["gy"]

    def whole(*args):
        plants = args[9].shape[0] // 8
        return jax.shard_map(
            functools.partial(shards, rows=rows, cols=cols, plants=plants),
            mesh=mesh,
            in_specs=(
                P(None, "gx", "gy", None),
                P(None, "gx", "gy", None),
                P(),
                P(),
                P("gx", "gy", None),
                P("gx", "gy", None, None),
                P("gx", "gy", None, None, None),
                P("gx", "gy", None),
                P("gx", "gy", None),
                P(),
            ),
            out_specs=(P("gx", "gy", None), P(("gx", "gy")), P(("gx", "gy"))),
            check_vma=False,
        )(*args)

    return whole
```

```python
import functools

import jax
import jax.numpy as jnp
from jax import lax
from jax.experimental import pallas as pl
from jax.experimental.pallas import tpu as pltpu
from jax.sharding import PartitionSpec as P

REACH = 2
SIDE = 2 * REACH + 1
SLOTS = SIDE * SIDE
HALVES = 2
PLANT_LANE = 64
MESH = pl.DeviceIdType.MESH
NT = (((1,), (1,)), ((), ()))


def nt_dot(left, right):
    return lax.dot_general(left, right, NT, preferred_element_type=jnp.float32)


def column(values, rows, width):
    index = lax.broadcasted_iota(jnp.int32, (rows, width), 0)
    out = jnp.full((rows, width), values[0], jnp.float32)
    for i in range(1, rows):
        out = jnp.where(index == i, values[i], out)
    return out


def kernel(
    rows, cols, organs, plants,
    direct, omega, band_sun_in, air_temp_in, vcmax_in, self_view, near_view, near_ids_in, organ_in, table_in,
    assim_ref, share_ref,
    views, own, tiles, msg1, msg0, recv1, recv0, msg2a, msg2b, recv2a, recv2b,
    table, plant_row, dest_org, dest_pl, lane_org, lane_pl, part, gathered,
    band_sun, air_temp, vcmax, near_ids, organ_ref,
    load_sem, small_sem, send1, got1, send0, got0, send2a, got2a, send2b, got2b, send3, got3,
):
    suns = direct.shape[0]
    bands = omega.shape[0]
    near = near_view.shape[2]
    width = vcmax.shape[-1]
    levels = table_in.shape[0]
    half = width // HALVES
    quarter = half // 4
    ndev = rows * cols
    row = lax.axis_index("gx")
    col = lax.axis_index("gy")
    me = row * cols + col

    own[suns + bands:, :] = jnp.zeros((own.shape[0] - suns - bands, width), jnp.float32)
    table[...] = jnp.zeros_like(table)
    pairs = [(direct.at[s, 0], own.at[pl.ds(s, 1)]) for s in range(suns)]
    pairs += [(omega.at[b, 0], own.at[pl.ds(suns + b, 1)]) for b in range(bands)]
    pairs += [
        (near_ids_in, near_ids), (organ_in, organ_ref), (table_in, table.at[pl.ds(0, levels)]),
        (vcmax_in, vcmax), (band_sun_in, band_sun), (air_temp_in, air_temp),
    ]
    smalls = [pltpu.make_async_copy(a, b, small_sem.at[i]) for i, (a, b) in enumerate(pairs)]
    for small in smalls:
        small.start()
    loads = {}
    for h, n in [(h, 0) for h in range(HALVES)] + [(h, n) for h in range(HALVES) for n in range(1, near + 1)]:
        span = pl.ds(h * half, half)
        source = self_view.at[0, 0, span] if n == 0 else near_view.at[0, 0, n - 1, span]
        loads[h, n] = pltpu.make_async_copy(source, views.at[n, span], load_sem.at[h, n])
        loads[h, n].start()

    barrier = pltpu.get_barrier_semaphore()

    def over_peers(act):
        for i in range(rows):
            r = lax.rem(row + i, rows)

            def step(j, carry, r=r):
                act(r, lax.rem(col + j, cols))
                return carry

            lax.fori_loop(1 if i == 0 else 0, cols, step, 0)

    over_peers(lambda r, c: pl.semaphore_signal(barrier, inc=1, device_id=(r, c), device_id_type=MESH))

    row_lo, row_hi = jnp.maximum(row - REACH, 0), jnp.minimum(row + REACH, rows - 1)
    col_lo, col_hi = jnp.maximum(col - REACH, 0), jnp.minimum(col + REACH, cols - 1)

    def each_neighbour(body):
        def by_row(r, carry):
            def by_col(c, inner):
                @pl.when((r != row) | (c != col))
                def _():
                    body(r, c)
                return inner
            return lax.fori_loop(col_lo, col_hi + 1, by_col, carry)
        lax.fori_loop(row_lo, row_hi + 1, by_row, 0)

    def exchange(message, slots, send_sem, got_sem, r, c, outgoing):
        there = (row - r + REACH) * SIDE + (col - c + REACH)
        here = (r - row + REACH) * SIDE + (c - col + REACH)
        return pltpu.make_async_remote_copy(
            src_ref=message, dst_ref=slots.at[there if outgoing else here],
            send_sem=send_sem.at[there], recv_sem=got_sem.at[there if outgoing else here],
            device_id=(r, c), device_id_type=MESH,
        )

    def send(*buffers):
        each_neighbour(lambda r, c: exchange(*buffers, r, c, True).start())

    def receive(*buffers):
        each_neighbour(lambda r, c: exchange(*buffers, r, c, False).wait_recv())

    def sent(*buffers):
        each_neighbour(lambda r, c: exchange(*buffers, r, c, True).wait_send())

    first = (msg1, recv1, send1, got1)
    albedos = (msg0, recv0, send0, got0)
    second = ((msg2a, recv2a, send2a, got2a), (msg2b, recv2b, send2b, got2b))

    def packed(values):
        step = values.shape[1] // 4
        return jnp.concatenate([values[:, i * step:(i + 1) * step] for i in range(4)], axis=0).astype(jnp.bfloat16)

    def unpacked(message):
        values = message.astype(jnp.float32)
        return jnp.concatenate([values[4 * i:4 * i + 4] for i in range(4)], axis=1)

    for small in smalls[:suns + bands]:
        small.wait()
    own_tile = own[...]
    msg1[...] = packed(own_tile[0:4])
    msg0[...] = packed(own_tile[4:8])

    pl.semaphore_wait(barrier, ndev - 1)
    send(*first)
    send(*albedos)
    for small in smalls[suns + bands:]:
        small.wait()

    entries = table[...]
    level = lax.broadcasted_iota(jnp.int32, entries.shape, 0)
    for j in range(width // 128):
        ids = organ_ref[0, :, j * 128:(j + 1) * 128]
        low = jnp.broadcast_to(ids & 127, entries.shape)
        picked = jnp.take_along_axis(entries, low, axis=1)
        picked = jnp.where(level == (ids >> 7), picked, 0).astype(jnp.float32)
        plant_row[:, j * 128:(j + 1) * 128] = jnp.sum(picked, axis=0, keepdims=True)
    for ids, total, base, dest_ref, lane_ref in (
        (organ_ref[0].astype(jnp.float32), organs, 0, dest_org, lane_org),
        (plant_row[...], plants, PLANT_LANE, dest_pl, lane_pl),
    ):
        share = total // ndev
        dest = jnp.floor((ids + 0.5) * (1.0 / share))
        lane = ids - dest * share + base
        at_row = lax.broadcasted_iota(jnp.int32, (ndev, width), 0).astype(jnp.float32)
        dest_ref[...] = jnp.where(at_row == dest, 1.0, 0.0)
        at_lane = lax.broadcasted_iota(jnp.int32, (128, width), 0).astype(jnp.float32)
        lane_ref[...] = jnp.where(at_lane == lane, 1.0, 0.0).astype(jnp.bfloat16)

    slot_of = []
    for n in range(near):
        block = near_ids[0, 0, n]
        place = (lax.div(block, cols) - row + REACH) * SIDE + (lax.rem(block, cols) - col + REACH)
        slot_of.append(jnp.clip(place, 0, SLOTS - 1))

    own_low = own_tile[0:suns].astype(jnp.bfloat16)
    totals = []
    for h in range(HALVES):
        loads[h, 0].wait()
        totals.append(nt_dot(own_low, views[0, h * half:(h + 1) * half, :]))
    receive(*first)
    for n in range(near):
        tiles[n, 0:4, :] = unpacked(recv1[slot_of[n]])
    once = []
    for h in range(HALVES):
        span = slice(h * half, (h + 1) * half)
        total = totals[h]
        for n in range(1, near + 1):
            loads[h, n].wait()
        for n in range(1, near + 1):
            total = total + nt_dot(tiles[n - 1, 0:4, :].astype(jnp.bfloat16), views[n, span, :])
        once.append(total)
        second[h][0][...] = packed(total)
        send(*second[h])

    def second_input(tile, h, light):
        span = slice(h * half, (h + 1) * half)
        scaled = [tile[suns + b:suns + b + 1, span] * light for b in range(bands)]
        scaled.append(jnp.zeros((16 - suns * bands, half), jnp.float32))
        return jnp.concatenate(scaled, axis=0).astype(jnp.bfloat16)

    twice = None
    for h in range(HALVES):
        term = nt_dot(second_input(own, h, once[h]), views[0, :, h * half:(h + 1) * half])
        twice = term if twice is None else twice + term
    receive(*albedos)
    for n in range(near):
        tiles[n, 4:8, :] = unpacked(recv0[slot_of[n]])
    for h in range(HALVES):
        receive(*second[h])
        for n in range(1, near + 1):
            light = unpacked(second[h][1][slot_of[n - 1]])
            twice = twice + nt_dot(second_input(tiles.at[n - 1], h, light), views[n, :, h * half:(h + 1) * half])

    base = own[0:suns, :] + jnp.concatenate(once, axis=1)
    absorbed = []
    for b in range(bands):
        factor = column([band_sun[b, s] for s in range(suns)], suns, width)
        gathered_light = factor * (base + twice[b * suns:(b + 1) * suns])
        absorbed.append((1.0 - own[suns + b:suns + b + 1, :]) * gathered_light)
    air = column([air_temp[s] for s in range(suns)], suns, width)
    leaf_temp = air + 6.0 * (absorbed[1] + absorbed[2])
    capacity = vcmax[0] * jnp.exp(0.07 * (leaf_temp - 25.0))
    jmax = 1.7 * capacity
    light = 1.5 * absorbed[0]
    total = light + jmax
    elec = (total - jnp.sqrt(total * total - 2.8 * light * jmax)) * (1.0 / 1.4)
    carbox = capacity * ((0.7 - 0.05) / (0.7 + 0.5))
    electron = elec * ((0.7 - 0.05) / (0.7 + 0.1))
    net_rate = jnp.minimum(carbox, electron) - 0.015 * capacity
    assim = 0.25 * jnp.sum(net_rate, axis=0, keepdims=True)
    assim_ref[0] = assim

    high = assim.astype(jnp.bfloat16).astype(jnp.float32)
    rest = assim - high
    middle = rest.astype(jnp.bfloat16).astype(jnp.float32)
    low = rest - middle
    sums = None
    for dest_ref, lane_ref in ((dest_org, lane_org), (dest_pl, lane_pl)):
        dest = dest_ref[...]
        stacked = jnp.concatenate([dest * high, dest * middle, dest * low], axis=0).astype(jnp.bfloat16)
        found = nt_dot(stacked, lane_ref[...])
        sums = found if sums is None else sums + found
    sums = sums[0:ndev] + sums[ndev:2 * ndev] + sums[2 * ndev:3 * ndev]
    part[...] = sums

    def hand(r, c):
        peer = r * cols + c
        pltpu.make_async_remote_copy(
            src_ref=part.at[pl.ds(peer, 1)], dst_ref=gathered.at[pl.ds(me, 1)],
            send_sem=send3, recv_sem=got3, device_id=(r, c), device_id_type=MESH,
        ).start()

    over_peers(hand)
    pltpu.make_async_copy(part.at[pl.ds(me, 1)], gathered.at[pl.ds(me, 1)], got3).start()
    sent(*first)
    sent(*albedos)
    sent(*second[0])
    sent(*second[1])
    pltpu.make_async_copy(part, gathered, got3).wait()
    share_ref[...] = jnp.sum(gathered[...], axis=0, keepdims=True)
    others = pl.ds(0, ndev - 1)
    pltpu.make_async_copy(part.at[others], gathered.at[others], send3).wait()


def finish(organ_share, plant_share, assim_in, share_in, assim_ref, organ_ref, plant_ref):
    assim_ref[...] = assim_in[...]
    organ_ref[...] = 0.25 * share_in[:, 0:organ_share]
    plant_ref[...] = share_in[:, PLANT_LANE:PLANT_LANE + plant_share] * (1.0 / 32.0)


def shards(
    direct, omega, band_sun, air_temp, vcmax, self_view, near_view, near_ids, organ_of_patch, organ_plant,
    *, rows, cols, plants,
):
    ndev = rows * cols
    organs = organ_plant.shape[0]
    near = near_ids.shape[-1]
    width = vcmax.shape[-1]
    levels = organs // 128
    padded = (levels + 7) // 8 * 8
    vmem = pl.BlockSpec(memory_space=pltpu.VMEM)
    hbm = pl.BlockSpec(memory_space=pl.ANY)
    f32, bf16 = jnp.float32, jnp.bfloat16
    slot_sems = pltpu.SemaphoreType.DMA((SLOTS,))
    assimilation, share = pl.pallas_call(
        functools.partial(kernel, rows, cols, organs, plants),
        out_shape=(
            jax.ShapeDtypeStruct((1, 1, width), f32),
            jax.ShapeDtypeStruct((1, 128), f32),
        ),
        in_specs=[hbm] * 10,
        out_specs=(vmem, vmem),
        scratch_shapes=[
            pltpu.VMEM((near + 1, width, width), bf16),
            pltpu.VMEM((8, width), f32),
            pltpu.VMEM((near, 8, width), f32),
            pltpu.VMEM((16, width // 4), bf16),
            pltpu.VMEM((16, width // 4), bf16),
            pltpu.VMEM((SLOTS, 16, width // 4), bf16),
            pltpu.VMEM((SLOTS, 16, width // 4), bf16),
            pltpu.VMEM((16, width // 8), bf16),
            pltpu.VMEM((16, width // 8), bf16),
            pltpu.VMEM((SLOTS, 16, width // 8), bf16),
            pltpu.VMEM((SLOTS, 16, width // 8), bf16),
            pltpu.VMEM((padded, 128), jnp.int32),
            pltpu.VMEM((1, width), f32),
            pltpu.VMEM((ndev, width), f32),
            pltpu.VMEM((ndev, width), f32),
            pltpu.VMEM((128, width), bf16),
            pltpu.VMEM((128, width), bf16),
            pltpu.VMEM((ndev, 128), f32),
            pltpu.VMEM((ndev, 128), f32),
            pltpu.SMEM(band_sun.shape, f32),
            pltpu.SMEM(air_temp.shape, f32),
            pltpu.VMEM(vcmax.shape, f32),
            pltpu.SMEM(near_ids.shape, jnp.int32),
            pltpu.VMEM(organ_of_patch.shape, jnp.int32),
            pltpu.SemaphoreType.DMA((HALVES, near + 1)),
            pltpu.SemaphoreType.DMA((16,)),
            slot_sems, slot_sems, slot_sems, slot_sems, slot_sems, slot_sems, slot_sems, slot_sems,
            pltpu.SemaphoreType.DMA, pltpu.SemaphoreType.DMA,
        ],
        compiler_params=pltpu.CompilerParams(
            collective_id=0, has_side_effects=True, vmem_limit_bytes=56 * 2**20
        ),
        name="canopy",
    )(
        direct, omega, band_sun, air_temp, vcmax, self_view, near_view, near_ids, organ_of_patch,
        organ_plant.reshape(levels, 128),
    )
    organ_share, plant_share = organs // ndev, plants // ndev
    assimilation, organ_carbon, plant_carbon = pl.pallas_call(
        functools.partial(finish, organ_share, plant_share),
        out_shape=(
            jax.ShapeDtypeStruct((1, 1, width), f32),
            jax.ShapeDtypeStruct((1, organ_share), f32),
            jax.ShapeDtypeStruct((1, plant_share), f32),
        ),
        in_specs=[vmem, vmem],
        out_specs=(vmem, vmem, vmem),
        compiler_params=pltpu.CompilerParams(vmem_limit_bytes=60 * 2**20),
        name="finish",
    )(assimilation, share)
    return assimilation, organ_carbon.reshape(-1), plant_carbon.reshape(-1)


def solution(mesh):
    rows, cols = mesh.shape["gx"], mesh.shape["gy"]

    def whole(*args):
        plants = args[9].shape[0] // 8
        return jax.shard_map(
            functools.partial(shards, rows=rows, cols=cols, plants=plants),
            mesh=mesh,
            in_specs=(
                P(None, "gx", "gy", None),
                P(None, "gx", "gy", None),
                P(),
                P(),
                P("gx", "gy", None),
                P("gx", "gy", None, None),
                P("gx", "gy", None, None, None),
                P("gx", "gy", None),
                P("gx", "gy", None),
                P(),
            ),
            out_specs=(P("gx", "gy", None), P(("gx", "gy")), P(("gx", "gy"))),
            check_vma=False,
        )(*args)

    return whole
```
